32 devices in a mesh: groups: 2 (over y), dp: 4 (over z), feat: 4 (over x, core).
Axes of the slice: x: 2, y: 2, z: 4, core: 2. Of those that a mesh axis runs over, the one named last changes fastest.
Arguments:
- train_feats: bfloat16 [4096, 8192], P('dp', 'feat'), may hold values from -6 to 6
- pool_feats: bfloat16 [64, 8192], P('dp', 'feat'), may hold values from -6 to 6
- kernel_inv: bfloat16 [8192, 8192], P('feat', 'dp')
- test_ids: int32 [384], P('groups'), parts along dimension 0, may hold values from 0 to 63
Outputs:
- scores: bfloat16 [4096, 384], P(('dp', 'feat'), 'groups'), parts along dimension 1
The draws below stay inside these ranges and needn't reach their ends.
There are 2 independent parts, one for each index of `groups`. The reference program is written for one: setup_inputs(seed, part) draws one part's arguments, and reference() takes and returns one part's arrays. A program takes and returns all parts, laid end to end along the dimension named above; an argument that names none is the same for every part. Nothing has to cross between parts.
All inputs are finite; a program needn't handle non-finite values.
Results may differ from the reference program's by a relative error of at most 0.0051.
Values may be sent and summed in bfloat16 or wider, within the bound.
A program may use at most 64 MiB of HBM per device.

```python
import jax
import jax.numpy as jnp

F = 8192
Q = 192
NTRAIN = 4096
POOL = 64


def draw_kernel_inv(key, part):
    key = jax.random.fold_in(key, 11)
    first, second = jax.random.split(key, 2)
    rows = jnp.arange(F)[:, None]
    cols = jnp.arange(F)[None, :]
    diag_vals = jnp.exp(jax.random.uniform(first, (F, 1), jnp.float32, 0.0, 2.302585)) * F ** (-0.5)
    off_diag = jax.random.normal(second, (F, F), jnp.float32) * (0.5 / F)
    whole = jnp.where(rows == cols, diag_vals, off_diag)
    return whole.astype(jnp.bfloat16)


def with_ends(values, stream_key, smallest, high):
    place = [jax.random.randint(jax.random.fold_in(stream_key, axis), (), 0, length) for axis, length in enumerate(values.shape)]
    main_axis = values.shape.index(max(values.shape))
    beside = place[:main_axis] + [(place[main_axis] + 1) % values.shape[main_axis]] + place[main_axis + 1:]
    return values.at[tuple(place)].set(smallest).at[tuple(beside)].set(high)


def block_scale(stream_key, shape, cuts, smallest, high):
    def one(dim, shards_of):
        draws = jax.random.uniform(jax.random.fold_in(jax.random.fold_in(stream_key, 6), dim), (shards_of,), jnp.float32, smallest / len(cuts), high / len(cuts))
        return jnp.repeat(jnp.exp(draws), shape[dim] // shards_of).reshape((-1,) + (1,) * (len(shape) - dim - 1))

    level = one(*cuts[0])
    for cut in cuts[1:]:
        level = level * one(*cut)
    return level


def centred(stream_key, extent, spread, reach, cuts=(), kind=jnp.bfloat16):
    entries = spread * jax.random.normal(stream_key, extent, jnp.float32)
    if cuts:
        entries = entries * block_scale(stream_key, extent, cuts, -0.22, 0.18)
    return jnp.clip(entries, -reach, reach).astype(kind)


def setup_inputs(seed: int = 0, part: int = 0) -> dict:
    key_list = jax.random.split(jax.random.key(seed), 5)
    part_splits = jax.random.split(jax.random.fold_in(key_list[4], part), 5)
    train_feats = centred(key_list[0], (NTRAIN, F), 1.0, 6.0, ((0, 4), (1, 4)))
    pool_feats = centred(key_list[1], (POOL, F), 1.0, 6.0, ((0, 4), (1, 4)))
    kernel_inv = draw_kernel_inv(jax.random.fold_in(key_list[4], 71), part)
    test_ids = with_ends(jax.random.randint(part_splits[3], (Q,), 0, POOL), jax.random.fold_in(part_splits[3], 1), 0, POOL - 1).astype(jnp.int32)
    return dict(train_feats=train_feats, pool_feats=pool_feats, kernel_inv=kernel_inv, test_ids=test_ids)


def reference(train_feats, pool_feats, kernel_inv, test_ids):
    test_rows = jnp.take(pool_feats, test_ids, axis=0)
    precond = jnp.dot(test_rows, kernel_inv, preferred_element_type=jnp.float32).astype(jnp.bfloat16)
    scores = jnp.dot(train_feats, precond.T, preferred_element_type=jnp.float32)
    return scores.astype(jnp.bfloat16)
```

```python
import functools

import jax
import jax.numpy as jnp
from jax import lax
from jax.experimental import pallas as pl
from jax.experimental.pallas import tpu as pltpu
from jax.sharding import PartitionSpec as P

MESH = pl.DeviceIdType.MESH
F32 = jnp.float32
BF16 = jnp.bfloat16
NT = (((1,), (1,)), ((), ()))
TN = (((0,), (0,)), ((), ()))


def per_device(train_feats, pool_feats, kernel_inv, test_ids):
    feat_width = train_feats.shape[1]
    whole_pool = lax.all_gather(pool_feats, "dp", axis=0, tiled=True)
    test_rows = jnp.take(whole_pool, test_ids, axis=0)
    partial_value = jnp.dot(test_rows, kernel_inv, preferred_element_type=F32)
    summed = lax.psum(partial_value, "feat").astype(BF16)
    every_col = lax.all_gather(summed, "dp", axis=1, tiled=True)
    start = lax.axis_index("feat") * feat_width
    precond = lax.dynamic_slice_in_dim(every_col, start, feat_width, 1)
    terms = lax.dot_general(train_feats, precond, NT, preferred_element_type=F32)
    mine = lax.psum_scatter(terms, "feat", scatter_dimension=0, tiled=True)
    return mine.astype(BF16)


def pick_columns(scores, ids, pool):
    rounded = scores.astype(BF16).astype(F32)
    finite = jnp.abs(rounded) <= float(jnp.finfo(BF16).max)
    value = jnp.where(finite, rounded, 0.0).astype(BF16)
    code = jnp.where(finite, 0.0, jnp.where(rounded > 0, 1.0, jnp.where(rounded < 0, 2.0, 3.0))).astype(BF16)
    places = lax.broadcasted_iota(jnp.int32, (pool, ids.shape[1]), 0)
    chosen = jnp.where(places == ids, 1.0, 0.0).astype(BF16)
    picked = lax.dot_general(value, chosen, TN, preferred_element_type=F32)
    codes = lax.dot_general(code, chosen, TN, preferred_element_type=F32)
    special = jnp.where(codes == 1.0, jnp.inf, jnp.where(codes == 2.0, -jnp.inf, jnp.nan))
    return jnp.where(codes == 0.0, picked, special).astype(BF16)


def kernel(
    train_hbm, pool_hbm, kinv_hbm, ids_hbm, out_ref,
    kinv, train, ids, pool, part1, got1, part2, got2, slices, precond, part3, got3, part4, got4,
    load_sem, pool_send, pool_recv, send1, recv1, send2, recv2, send3, recv3, send4, recv4, send5, recv5, send6, recv6,
):
    g, d, f = lax.axis_index("groups"), lax.axis_index("dp"), lax.axis_index("feat")
    x, c = f // 2, f % 2
    depth, width = kinv.shape[1], kinv.shape[2]
    pool_rows = pool.shape[0] * pool.shape[1]
    sibling = (g, d, 2 * x + 1 - c)
    around = [(1 - g, 1 - x), (1 - g, x), (g, 1 - x), (g, x)]
    me = c * 4 + g * 2 + x

    def remote(src, dst, send, recv, device):
        return pltpu.make_async_remote_copy(
            src_ref=src, dst_ref=dst, send_sem=send, recv_sem=recv, device_id=device, device_id_type=MESH
        )

    loads = []

    def load(src, dst):
        copy = pltpu.make_async_copy(src, dst, load_sem.at[len(loads)])
        copy.start()
        loads.append(copy)
        return copy

    depth_from = pl.multiple_of(g * depth, depth)
    pool_half = pool_hbm.at[:, pl.ds(depth_from, depth)]
    own_pool = load(pool_half, pool.at[d])
    kinv_loads = []
    for i in range(8):
        core = 1 - c if i < 4 else c
        gg, xx = around[i % 4]
        col = pl.multiple_of((core * 4 + gg * 2 + xx) * width, width)
        kinv_loads.append(load(kinv_hbm.at[pl.ds(depth_from, depth), pl.ds(col, width)], kinv.at[i]))
    train_loads = [
        load(train_hbm.at[pl.ds(i * train.shape[1], train.shape[1]), :], train.at[i]) for i in range(4)
    ]
    ids_load = load(ids_hbm, ids)

    barrier = pltpu.get_barrier_semaphore()
    for r in range(1, 4):
        pl.semaphore_signal(barrier, inc=1, device_id=(g, (d + r) % 4, f), device_id_type=MESH)
    for r in range(4):
        for gg in (g, 1 - g) if r else (1 - g,):
            pl.semaphore_signal(barrier, inc=1, device_id=(gg, d, (f + r) % 4), device_id_type=MESH)
    pl.semaphore_wait(barrier, 10)

    sends = []

    pool_copies = []
    for r in range(1, 4):
        copy = remote(pool_half, pool.at[d], pool_send.at[r], pool_recv.at[r], (g, (d + r) % 4, f))
        copy.start()
        pool_copies.append(copy)
    own_pool.wait()
    for copy in pool_copies:
        copy.wait_recv()
    rows = pool[...].reshape(pool_rows, depth)

    copies1 = []
    for i in range(4):
        kinv_loads[i].wait()
        part1[i] = jnp.dot(rows, kinv[i], preferred_element_type=F32)
        copy = remote(part1.at[i], got1.at[i], send1.at[i], recv1.at[i], sibling)
        copy.start()
        copies1.append(copy)
    copies2 = []
    for i in range(4):
        kinv_loads[4 + i].wait()
        term = jnp.dot(rows, kinv[4 + i], preferred_element_type=F32)
        copies1[i].wait_recv()
        part2[i] = term + got1[i]
        if i < 3:
            gg, xx = around[i]
            copy = remote(part2.at[i], got2.at[i], send2.at[i], recv2.at[i], (gg, d, 2 * xx + c))
            copy.start()
            copies2.append(copy)
    total = part2[3]
    for i in (2, 1, 0):
        copies2[i].wait_recv()
        total = total + got2[i]
    slices[d] = total.astype(BF16)

    copies3 = []
    for r in range(1, 4):
        copy = remote(slices.at[d], slices.at[d], send3.at[r], recv3.at[r], (g, (d + r) % 4, f))
        copy.start()
        copies3.append(copy)

    col = pl.multiple_of(me * width, width)

    def forward(n, j):
        mine = precond.at[:, pl.ds(col, width)]
        across = remote(slices.at[j], mine, send4.at[n, 1], recv4.at[me], (1 - g, d, j))
        beside = remote(slices.at[j], mine, send4.at[n, 0], recv4.at[me], (g, d, j))
        across.start()

        @pl.when(f != j)
        def _():
            beside.start()

        @pl.when(f == j)
        def _():
            precond[:, pl.ds(col, width)] = slices[j]

        return across, beside, j

    forwards = [forward(0, d)]
    for r in range(1, 4):
        copies3[r - 1].wait_recv()
        forwards.append(forward(r, (d - r + 4) % 4))
    for r in range(1, 8):
        k = (me + r) % 8
        other = precond.at[:, pl.ds(pl.multiple_of(k * width, width), width)]
        pltpu.make_async_remote_copy(
            src_ref=other, dst_ref=other, send_sem=send4.at[0, 0], recv_sem=recv4.at[k],
            device_id=sibling, device_id_type=MESH,
        ).wait_recv()

    for copy in train_loads:
        copy.wait()
    left = precond[...]

    def term(j):
        return lax.dot_general(left, train[j], NT, preferred_element_type=F32)

    copies5 = []
    for i, xx in enumerate((1 - x, x)):
        part3[i] = term(2 * xx + 1 - c)
        copy = remote(part3.at[i], got3.at[i], send5.at[i], recv5.at[i], sibling)
        copy.start()
        copies5.append(copy)
    first = term(2 * (1 - x) + c)
    copies5[0].wait_recv()
    part4[...] = first + got3[0]
    copy6 = remote(part4, got4, send6, recv6, (g, d, 2 * (1 - x) + c))
    copy6.start()
    second = term(f)
    copies5[1].wait_recv()
    second = second + got3[1]
    ids_load.wait()
    copy6.wait_recv()
    out_ref[...] = pick_columns(second + got4[...], ids[...], pool_rows)

    for copy in pool_copies + copies1 + copies2 + copies3 + copies5 + [copy6]:
        copy.wait_send()
    for across, beside, j in forwards:
        across.wait_send()

        @pl.when(f != j)
        def _(beside=beside):
            beside.wait_send()


def fused(train_feats, pool_feats, kernel_inv, test_ids):
    rows, feats = train_feats.shape
    pool_block = pool_feats.shape[0]
    pool_rows = 4 * pool_block
    depth, width = feats // 2, kernel_inv.shape[1] // 8
    out_rows = rows // 4
    queries = test_ids.shape[0]
    dma = pltpu.SemaphoreType.DMA
    return pl.pallas_call(
        kernel,
        out_shape=jax.ShapeDtypeStruct((out_rows, queries), BF16),
        in_specs=[pl.BlockSpec(memory_space=pl.ANY)] * 4,
        out_specs=pl.BlockSpec(memory_space=pltpu.VMEM),
        scratch_shapes=[
            pltpu.VMEM((8, depth, width), BF16),
            pltpu.VMEM((4, out_rows, feats), BF16),
            pltpu.VMEM((1, queries), jnp.int32),
            pltpu.VMEM((4, pool_block, depth), BF16),
            pltpu.VMEM((4, pool_rows, width), F32),
            pltpu.VMEM((4, pool_rows, width), F32),
            pltpu.VMEM((4, pool_rows, width), F32),
            pltpu.VMEM((3, pool_rows, width), F32),
            pltpu.VMEM((4, pool_rows, width), BF16),
            pltpu.VMEM((pool_rows, 8 * width), BF16),
            pltpu.VMEM((2, pool_rows, out_rows), F32),
            pltpu.VMEM((2, pool_rows, out_rows), F32),
            pltpu.VMEM((pool_rows, out_rows), F32),
            pltpu.VMEM((pool_rows, out_rows), F32),
            dma((14,)), dma((4,)), dma((4,)), dma((4,)), dma((4,)), dma((3,)), dma((3,)),
            dma((4,)), dma((4,)), dma((4, 2)), dma((8,)), dma((2,)), dma((2,)), dma, dma,
        ],
        compiler_params=pltpu.CompilerParams(
            collective_id=0, has_side_effects=True, vmem_limit_bytes=48 * 1024 * 1024
        ),
        cost_estimate=pl.CostEstimate(
            flops=2 * pool_rows * feats * (kernel_inv.shape[1] // 2 + rows),
            bytes_accessed=2 * (train_feats.size + kernel_inv.size // 2 + out_rows * queries),
            transcendentals=0,
        ),
    )(train_feats, pool_feats, kernel_inv, test_ids.reshape(1, queries))


def solution(mesh):
    sizes = tuple(mesh.shape[name] for name in ("groups", "dp", "feat"))

    def body(train_feats, pool_feats, kernel_inv, test_ids):
        pool_rows = sizes[1] * pool_feats.shape[0]
        square = train_feats.shape[1] == kernel_inv.shape[1]
        if sizes == (2, 4, 4) and square and pool_rows <= test_ids.shape[0]:
            return fused(train_feats, pool_feats, kernel_inv, test_ids)
        return per_device(train_feats, pool_feats, kernel_inv, test_ids)

    placed = (P("dp", "feat"), P("dp", "feat"), P("feat", "dp"), P("groups"))
    return jax.shard_map(
        body,
        mesh=mesh,
        in_specs=placed,
        out_specs=P(("dp", "feat"), "groups"),
        check_vma=False,
    )
```

```python
import functools

import jax
import jax.numpy as jnp
from jax import lax
from jax.experimental import pallas as pl
from jax.experimental.pallas import tpu as pltpu
from jax.sharding import PartitionSpec as P

MESH = pl.DeviceIdType.MESH
F32 = jnp.float32
BF16 = jnp.bfloat16
NT = (((1,), (1,)), ((), ()))
TN = (((0,), (0,)), ((), ()))


def per_device(train_feats, pool_feats, kernel_inv, test_ids):
    feat_width = train_feats.shape[1]
    whole_pool = lax.all_gather(pool_feats, "dp", axis=0, tiled=True)
    test_rows = jnp.take(whole_pool, test_ids, axis=0)
    partial_value = jnp.dot(test_rows, kernel_inv, preferred_element_type=F32)
    summed = lax.psum(partial_value, "feat").astype(BF16)
    every_col = lax.all_gather(summed, "dp", axis=1, tiled=True)
    start = lax.axis_index("feat") * feat_width
    precond = lax.dynamic_slice_in_dim(every_col, start, feat_width, 1)
    terms = lax.dot_general(train_feats, precond, NT, preferred_element_type=F32)
    mine = lax.psum_scatter(terms, "feat", scatter_dimension=0, tiled=True)
    return mine.astype(BF16)


def pick_columns(scores, ids, pool):
    rounded = scores.astype(BF16).astype(F32)
    finite = jnp.abs(rounded) <= float(jnp.finfo(BF16).max)
    value = jnp.where(finite, rounded, 0.0).astype(BF16)
    code = jnp.where(finite, 0.0, jnp.where(rounded > 0, 1.0, jnp.where(rounded < 0, 2.0, 3.0))).astype(BF16)
    places = lax.broadcasted_iota(jnp.int32, (pool, ids.shape[1]), 0)
    chosen = jnp.where(places == ids, 1.0, 0.0).astype(BF16)
    picked = lax.dot_general(value, chosen, TN, preferred_element_type=F32)
    codes = lax.dot_general(code, chosen, TN, preferred_element_type=F32)
    special = jnp.where(codes == 1.0, jnp.inf, jnp.where(codes == 2.0, -jnp.inf, jnp.nan))
    return jnp.where(codes == 0.0, picked, special).astype(BF16)


def kernel(
    train_hbm, pool_hbm, kinv_hbm, ids_hbm, out_ref,
    kinv, train, ids, pool, part1, got1, part2, got2, mine, precond, part3, got3, part4, got4,
    load_sem, pool_send, pool_recv, send1, recv1, send2, recv2, send3, recv3, send4, recv4, send5, recv5,
):
    g, d, f = lax.axis_index("groups"), lax.axis_index("dp"), lax.axis_index("feat")
    x, c = f // 2, f % 2
    depth, width = kinv.shape[1], kinv.shape[2]
    pool_rows = pool.shape[0] * pool.shape[1]
    sibling = (g, d, 2 * x + 1 - c)
    around = [(1 - g, 1 - x), (1 - g, x), (g, 1 - x), (g, x)]
    held = train.shape[2]

    def remote(src, dst, send, recv, device):
        return pltpu.make_async_remote_copy(
            src_ref=src, dst_ref=dst, send_sem=send, recv_sem=recv, device_id=device, device_id_type=MESH
        )

    loads = []

    def load(src, dst):
        copy = pltpu.make_async_copy(src, dst, load_sem.at[len(loads)])
        copy.start()
        loads.append(copy)
        return copy

    depth_from = pl.multiple_of(g * depth, depth)
    pool_half = pool_hbm.at[:, pl.ds(depth_from, depth)]
    own_pool = load(pool_half, pool.at[d])
    kinv_loads = []
    for i in range(8):
        core = 1 - c if i < 4 else c
        gg, xx = around[i % 4]
        col = pl.multiple_of((gg * 4 + 2 * xx + core) * width, width)
        kinv_loads.append(load(kinv_hbm.at[pl.ds(depth_from, depth), pl.ds(col, width)], kinv.at[i]))
    train_loads = [
        load(
            train_hbm.at[pl.ds(i * train.shape[1], train.shape[1]), pl.ds(pl.multiple_of(g * held, held), held)],
            train.at[i],
        )
        for i in range(4)
    ]
    ids_load = load(ids_hbm, ids)

    barrier = pltpu.get_barrier_semaphore()
    for r in range(1, 4):
        pl.semaphore_signal(barrier, inc=1, device_id=(g, (d + r) % 4, f), device_id_type=MESH)
    for r in range(4):
        for gg in (g, 1 - g) if r else (1 - g,):
            pl.semaphore_signal(barrier, inc=1, device_id=(gg, d, (f + r) % 4), device_id_type=MESH)

    @pl.when(f != d)
    def _():
        for r in range(1, 4):
            pl.semaphore_signal(barrier, inc=1, device_id=(g, f, (f + r) % 4), device_id_type=MESH)
        pl.semaphore_wait(barrier, 13)

    @pl.when(f == d)
    def _():
        pl.semaphore_wait(barrier, 10)

    pool_copies = []
    for r in range(1, 4):
        copy = remote(pool_half, pool.at[d], pool_send.at[r], pool_recv.at[r], (g, (d + r) % 4, f))
        copy.start()
        pool_copies.append(copy)
    own_pool.wait()
    for copy in pool_copies:
        copy.wait_recv()
    rows = pool[...].reshape(pool_rows, depth)

    copies1 = []
    for i in range(4):
        kinv_loads[i].wait()
        part1[i] = jnp.dot(rows, kinv[i], preferred_element_type=F32)
        copy = remote(part1.at[i], got1.at[i], send1.at[i], recv1.at[i], sibling)
        copy.start()
        copies1.append(copy)
    copies2 = []
    for i in range(4):
        kinv_loads[4 + i].wait()
        term = jnp.dot(rows, kinv[4 + i], preferred_element_type=F32)
        copies1[i].wait_recv()
        part2[i] = term + got1[i]
        if i < 3:
            gg, xx = around[i]
            copy = remote(part2.at[i], got2.at[i], send2.at[i], recv2.at[i], (gg, d, 2 * xx + c))
            copy.start()
            copies2.append(copy)
    total = part2[3]
    for i in (2, 1, 0):
        copies2[i].wait_recv()
        total = total + got2[i]
    mine[...] = total.astype(BF16)

    here = pl.multiple_of(f * width, width)
    copies3 = []
    for r in range(4):
        target = (g, (d + r) % 4, d)
        copies3.append(remote(mine, precond.at[:, pl.ds(here, width)], send3.at[r], recv3.at[f], target))
    for r in (2, 1, 3):
        copies3[r].start()

    @pl.when(f != d)
    def _():
        copies3[0].start()

    @pl.when(f == d)
    def _():
        precond[:, pl.ds(here, width)] = mine[...]

    for copy in train_loads:
        copy.wait()
    ids_load.wait()
    for r in range(4):
        source = (f + r) % 4
        place = precond.at[:, pl.ds(pl.multiple_of(source * width, width), width)]
        arrival = remote(mine, place, send3.at[0], recv3.at[source], sibling)
        if r:
            arrival.wait_recv()
        else:
            pl.when(f != d)(arrival.wait_recv)

    left = precond[...]

    def term(j):
        return lax.dot_general(left, train[j], NT, preferred_element_type=F32)

    copies4 = []
    for i, xx in enumerate((1 - x, x)):
        part3[i] = term(2 * xx + 1 - c)
        copy = remote(part3.at[i], got3.at[i], send4.at[i], recv4.at[i], sibling)
        copy.start()
        copies4.append(copy)
    terms = [term(2 * xx + c) for xx in (1 - x, x)]
    copies5 = []
    for i in range(2):
        copies4[i].wait_recv()
        part4[i] = terms[i] + got3[i]
        for gg, xx in around[:1] + around[2:3] if i == 0 else around[1:2]:
            n = len(copies5)
            copy = remote(part4.at[i], got4.at[n], send5.at[n], recv5.at[n], (gg, d, 2 * xx + c))
            copy.start()
            copies5.append(copy)
    total = part4[1]
    for n in (2, 1, 0):
        copies5[n].wait_recv()
        total = total + got4[n]
    out_ref[...] = pick_columns(total, ids[...], pool_rows)

    for copy in pool_copies + copies1 + copies2 + copies3[1:] + copies4 + copies5:
        copy.wait_send()
    pl.when(f != d)(copies3[0].wait_send)


def fused(train_feats, pool_feats, kernel_inv, test_ids):
    rows, feats = train_feats.shape
    pool_block = pool_feats.shape[0]
    pool_rows = 4 * pool_block
    depth, width = feats // 2, kernel_inv.shape[1] // 8
    out_rows = rows // 4
    queries = test_ids.shape[0]
    dma = pltpu.SemaphoreType.DMA
    held_in_hbm = (train_feats, pool_feats, kernel_inv, test_ids.reshape(1, queries))
    return pl.pallas_call(
        kernel,
        out_shape=jax.ShapeDtypeStruct((out_rows, queries), BF16),
        in_specs=[pl.BlockSpec(memory_space=pl.ANY)] * 4,
        out_specs=pl.BlockSpec(memory_space=pltpu.VMEM),
        scratch_shapes=[
            pltpu.VMEM((8, depth, width), BF16),
            pltpu.VMEM((4, out_rows, depth), BF16),
            pltpu.VMEM((1, queries), jnp.int32),
            pltpu.VMEM((4, pool_block, depth), BF16),
            pltpu.VMEM((4, pool_rows, width), F32),
            pltpu.VMEM((4, pool_rows, width), F32),
            pltpu.VMEM((4, pool_rows, width), F32),
            pltpu.VMEM((3, pool_rows, width), F32),
            pltpu.VMEM((pool_rows, width), BF16),
            pltpu.VMEM((pool_rows, 4 * width), BF16),
            pltpu.VMEM((2, pool_rows, out_rows), F32),
            pltpu.VMEM((2, pool_rows, out_rows), F32),
            pltpu.VMEM((2, pool_rows, out_rows), F32),
            pltpu.VMEM((3, pool_rows, out_rows), F32),
            dma((14,)), dma((4,)), dma((4,)), dma((4,)), dma((4,)), dma((3,)), dma((3,)),
            dma((4,)), dma((4,)), dma((2,)), dma((2,)), dma((3,)), dma((3,)),
        ],
        compiler_params=pltpu.CompilerParams(
            collective_id=0, has_side_effects=True, vmem_limit_bytes=48 * 1024 * 1024
        ),
        cost_estimate=pl.CostEstimate(
            flops=2 * pool_rows * feats * (kernel_inv.shape[1] + rows) // 2,
            bytes_accessed=train_feats.size + kernel_inv.size + 2 * out_rows * queries,
            transcendentals=0,
        ),
    )(*[pltpu.with_memory_space_constraint(held, pltpu.HBM) for held in held_in_hbm])


def solution(mesh):
    sizes = tuple(mesh.shape[name] for name in ("groups", "dp", "feat"))

    def body(train_feats, pool_feats, kernel_inv, test_ids):
        pool_rows = sizes[1] * pool_feats.shape[0]
        square = train_feats.shape[1] == kernel_inv.shape[1]
        if sizes == (2, 4, 4) and square and pool_rows <= test_ids.shape[0]:
            return fused(train_feats, pool_feats, kernel_inv, test_ids)
        return per_device(train_feats, pool_feats, kernel_inv, test_ids)

    placed = (P("dp", "feat"), P("dp", "feat"), P("feat", "dp"), P("groups"))
    return jax.shard_map(
        body,
        mesh=mesh,
        in_specs=placed,
        out_specs=P(("dp", "feat"), "groups"),
        check_vma=False,
    )
```

```python
import functools

import jax
import jax.numpy as jnp
from jax import lax
from jax.experimental import pallas as pl
from jax.experimental.pallas import tpu as pltpu
from jax.sharding import PartitionSpec as P

MESH = pl.DeviceIdType.MESH
F32 = jnp.float32
BF16 = jnp.bfloat16
NT = (((1,), (1,)), ((), ()))
TN = (((0,), (0,)), ((), ()))


def per_device(train_feats, pool_feats, kernel_inv, test_ids):
    feat_width = train_feats.shape[1]
    whole_pool = lax.all_gather(pool_feats, "dp", axis=0, tiled=True)
    test_rows = jnp.take(whole_pool, test_ids, axis=0)
    partial_value = jnp.dot(test_rows, kernel_inv, preferred_element_type=F32)
    summed = lax.psum(partial_value, "feat").astype(BF16)
    every_col = lax.all_gather(summed, "dp", axis=1, tiled=True)
    start = lax.axis_index("feat") * feat_width
    precond = lax.dynamic_slice_in_dim(every_col, start, feat_width, 1)
    terms = lax.dot_general(train_feats, precond, NT, preferred_element_type=F32)
    mine = lax.psum_scatter(terms, "feat", scatter_dimension=0, tiled=True)
    return mine.astype(BF16)


def pick_columns(scores, ids, pool):
    rounded = scores.astype(BF16).astype(F32)
    finite = jnp.abs(rounded) <= float(jnp.finfo(BF16).max)
    value = jnp.where(finite, rounded, 0.0).astype(BF16)
    code = jnp.where(finite, 0.0, jnp.where(rounded > 0, 1.0, jnp.where(rounded < 0, 2.0, 3.0))).astype(BF16)
    places = lax.broadcasted_iota(jnp.int32, (pool, ids.shape[1]), 0)
    chosen = jnp.where(places == ids, 1.0, 0.0).astype(BF16)
    picked = lax.dot_general(value, chosen, TN, preferred_element_type=F32)
    codes = lax.dot_general(code, chosen, TN, preferred_element_type=F32)
    special = jnp.where(codes == 1.0, jnp.inf, jnp.where(codes == 2.0, -jnp.inf, jnp.nan))
    return jnp.where(codes == 0.0, picked, special).astype(BF16)


def kernel(
    train_hbm, pool_hbm, kinv_hbm, ids_hbm, out_ref,
    kinv, train, ids, pool, part1, got1, part2, got2, mine, precond, part3, got3, part4, got4,
    load_sem, pool_send, pool_recv, send1, recv1, send2, recv2, send3, recv3, send4, recv4, send5, recv5,
):
    g, d, f = lax.axis_index("groups"), lax.axis_index("dp"), lax.axis_index("feat")
    x, c = f // 2, f % 2
    depth, width = kinv.shape[1], kinv.shape[2]
    pool_rows = pool.shape[0] * pool.shape[1]
    sibling = (g, d, 2 * x + 1 - c)
    around = [(1 - g, 1 - x), (1 - g, x), (g, 1 - x), (g, x)]
    held = train.shape[2]

    def remote(src, dst, send, recv, device):
        return pltpu.make_async_remote_copy(
            src_ref=src, dst_ref=dst, send_sem=send, recv_sem=recv, device_id=device, device_id_type=MESH
        )

    loads = []

    def load(src, dst):
        copy = pltpu.make_async_copy(src, dst, load_sem.at[len(loads)])
        copy.start()
        loads.append(copy)
        return copy

    depth_from = pl.multiple_of(g * depth, depth)
    pool_half = pool_hbm.at[:, pl.ds(depth_from, depth)]
    own_pool = load(pool_half, pool.at[d])
    kinv_loads = []
    for i in range(8):
        core = 1 - c if i < 4 else c
        gg, xx = around[i % 4]
        col = pl.multiple_of((gg * 4 + 2 * xx + core) * width, width)
        kinv_loads.append(load(kinv_hbm.at[pl.ds(depth_from, depth), pl.ds(col, width)], kinv.at[i]))
    train_loads = [
        load(
            train_hbm.at[pl.ds(i * train.shape[1], train.shape[1]), pl.ds(pl.multiple_of(g * held, held), held)],
            train.at[i],
        )
        for i in range(4)
    ]
    ids_load = load(ids_hbm, ids)

    barrier = pltpu.get_barrier_semaphore()
    for r in range(1, 4):
        pl.semaphore_signal(barrier, inc=1, device_id=(g, (d + r) % 4, f), device_id_type=MESH)
    for r in range(4):
        for gg in (g, 1 - g) if r else (1 - g,):
            pl.semaphore_signal(barrier, inc=1, device_id=(gg, d, (f + r) % 4), device_id_type=MESH)
    pl.semaphore_wait(barrier, 10)

    own_pool.wait()
    outward = 1 - 2 * (d // 2)
    pool_copies = []
    for r in (3, 2, 1):
        target = (g, (d + 4 + outward * r) % 4, f)
        copy = remote(pool.at[d], pool.at[d], pool_send.at[r], pool_recv.at[d], target)
        copy.start()
        pool_copies.append(copy)
    for r in (1, 2, 3):
        source = (d + r) % 4
        remote(pool.at[source], pool.at[source], pool_send.at[r], pool_recv.at[source], sibling).wait_recv()
    rows = pool[...].reshape(pool_rows, depth)

    copies1 = []
    for i in range(4):
        kinv_loads[i].wait()
        part1[i] = jnp.dot(rows, kinv[i], preferred_element_type=F32)
        copy = remote(part1.at[i], got1.at[i], send1.at[i], recv1.at[i], sibling)
        copy.start()
        copies1.append(copy)
    copies2 = []
    for i in range(4):
        kinv_loads[4 + i].wait()
        term = jnp.dot(rows, kinv[4 + i], preferred_element_type=F32)
        copies1[i].wait_recv()
        both = term + got1[i]
        if i == 3:
            total = both
        else:
            part2[i] = both.astype(BF16)
        if i < 3:
            gg, xx = around[i]
            copy = remote(part2.at[i], got2.at[i], send2.at[i], recv2.at[i], (gg, d, 2 * xx + c))
            copy.start()
            copies2.append(copy)
    for i in (2, 1, 0):
        copies2[i].wait_recv()
        total = total + got2[i].astype(F32)
    mine[...] = total.astype(BF16)

    here = pl.multiple_of(f * width, width)
    copies3 = []
    for r in range(4):
        target = (g, (d + r) % 4, d)
        copies3.append(remote(mine, precond.at[:, pl.ds(here, width)], send3.at[r], recv3.at[f], target))
    for r in (2, 1, 3):
        copies3[r].start()

    @pl.when(f != d)
    def _():
        copies3[0].start()

    @pl.when(f == d)
    def _():
        precond[:, pl.ds(here, width)] = mine[...]

    for copy in train_loads:
        copy.wait()
    ids_load.wait()

    for r in range(4):
        source = (f + r) % 4
        place = precond.at[:, pl.ds(pl.multiple_of(source * width, width), width)]
        arrival = remote(mine, place, send3.at[0], recv3.at[source], sibling)
        if r:
            arrival.wait_recv()
        else:
            pl.when(f != d)(arrival.wait_recv)

    left = precond[...]

    def term(j):
        return lax.dot_general(left, train[j], NT, preferred_element_type=F32)

    copies4 = []
    for i, xx in enumerate((1 - x, x)):
        part3[i] = term(2 * xx + 1 - c)
        copy = remote(part3.at[i], got3.at[i], send4.at[i], recv4.at[i], sibling)
        copy.start()
        copies4.append(copy)
    terms = [term(2 * xx + c) for xx in (1 - x, x)]
    copies5 = []
    for i in range(2):
        copies4[i].wait_recv()
        both = terms[i] + got3[i]
        part4[i] = both.astype(BF16)
        for gg, xx in around[:1] + around[2:3] if i == 0 else around[1:2]:
            n = len(copies5)
            copy = remote(part4.at[i], got4.at[n], send5.at[n], recv5.at[n], (gg, d, 2 * xx + c))
            copy.start()
            copies5.append(copy)
    total = both
    for n in (2, 1, 0):
        copies5[n].wait_recv()
        total = total + got4[n].astype(F32)
    out_ref[...] = pick_columns(total, ids[...], pool_rows)

    for copy in pool_copies + copies1 + copies2 + copies3[1:] + copies4 + copies5:
        copy.wait_send()
    pl.when(f != d)(copies3[0].wait_send)


def fused(train_feats, pool_feats, kernel_inv, test_ids):
    rows, feats = train_feats.shape
    pool_block = pool_feats.shape[0]
    pool_rows = 4 * pool_block
    depth, width = feats // 2, kernel_inv.shape[1] // 8
    out_rows = rows // 4
    queries = test_ids.shape[0]
    dma = pltpu.SemaphoreType.DMA
    held_in_hbm = (train_feats, pool_feats, kernel_inv, test_ids.reshape(1, queries))
    return pl.pallas_call(
        kernel,
        out_shape=jax.ShapeDtypeStruct((out_rows, queries), BF16),
        in_specs=[pl.BlockSpec(memory_space=pl.ANY)] * 4,
        out_specs=pl.BlockSpec(memory_space=pltpu.VMEM),
        scratch_shapes=[
            pltpu.VMEM((8, depth, width), BF16),
            pltpu.VMEM((4, out_rows, depth), BF16),
            pltpu.VMEM((1, queries), jnp.int32),
            pltpu.VMEM((4, pool_block, depth), BF16),
            pltpu.VMEM((4, pool_rows, width), F32),
            pltpu.VMEM((4, pool_rows, width), F32),
            pltpu.VMEM((4, pool_rows, width), BF16),
            pltpu.VMEM((3, pool_rows, width), BF16),
            pltpu.VMEM((pool_rows, width), BF16),
            pltpu.VMEM((pool_rows, 4 * width), BF16),
            pltpu.VMEM((4, pool_rows, out_rows), F32),
            pltpu.VMEM((2, pool_rows, out_rows), F32),
            pltpu.VMEM((2, pool_rows, out_rows), BF16),
            pltpu.VMEM((3, pool_rows, out_rows), BF16),
            dma((14,)), dma((4,)), dma((4,)), dma((4,)), dma((4,)), dma((3,)), dma((3,)),
            dma((4,)), dma((4,)), dma((2,)), dma((2,)), dma((3,)), dma((3,)),
        ],
        compiler_params=pltpu.CompilerParams(
            collective_id=0, has_side_effects=True, vmem_limit_bytes=48 * 1024 * 1024
        ),
        cost_estimate=pl.CostEstimate(
            flops=2 * pool_rows * feats * (kernel_inv.shape[1] + rows) // 2,
            bytes_accessed=train_feats.size + kernel_inv.size + 2 * out_rows * queries,
            transcendentals=0,
        ),
    )(*[pltpu.with_memory_space_constraint(held, pltpu.HBM) for held in held_in_hbm])


def solution(mesh):
    sizes = tuple(mesh.shape[name] for name in ("groups", "dp", "feat"))

    def body(train_feats, pool_feats, kernel_inv, test_ids):
        pool_rows = sizes[1] * pool_feats.shape[0]
        square = train_feats.shape[1] == kernel_inv.shape[1]
        if sizes == (2, 4, 4) and square and pool_rows <= test_ids.shape[0]:
            return fused(train_feats, pool_feats, kernel_inv, test_ids)
        return per_device(train_feats, pool_feats, kernel_inv, test_ids)

    placed = (P("dp", "feat"), P("dp", "feat"), P("feat", "dp"), P("groups"))
    return jax.shard_map(
        body,
        mesh=mesh,
        in_specs=placed,
        out_specs=P(("dp", "feat"), "groups"),
        check_vma=False,
    )
```

```python
import functools

import jax
import jax.numpy as jnp
from jax import lax
from jax.experimental import pallas as pl
from jax.experimental.pallas import tpu as pltpu
from jax.sharding import PartitionSpec as P

MESH = pl.DeviceIdType.MESH
F32 = jnp.float32
BF16 = jnp.bfloat16
NT = (((1,), (1,)), ((), ()))
TN = (((0,), (0,)), ((), ()))


def per_device(train_feats, pool_feats, kernel_inv, test_ids):
    feat_width = train_feats.shape[1]
    whole_pool = lax.all_gather(pool_feats, "dp", axis=0, tiled=True)
    test_rows = jnp.take(whole_pool, test_ids, axis=0)
    partial_value = jnp.dot(test_rows, kernel_inv, preferred_element_type=F32)
    summed = lax.psum(partial_value, "feat").astype(BF16)
    every_col = lax.all_gather(summed, "dp", axis=1, tiled=True)
    start = lax.axis_index("feat") * feat_width
    precond = lax.dynamic_slice_in_dim(every_col, start, feat_width, 1)
    terms = lax.dot_general(train_feats, precond, NT, preferred_element_type=F32)
    mine = lax.psum_scatter(terms, "feat", scatter_dimension=0, tiled=True)
    return mine.astype(BF16)


def pick_columns(scores, ids, pool):
    rounded = scores.astype(BF16).astype(F32)
    finite = jnp.abs(rounded) <= float(jnp.finfo(BF16).max)
    value = jnp.where(finite, rounded, 0.0).astype(BF16)
    code = jnp.where(finite, 0.0, jnp.where(rounded > 0, 1.0, jnp.where(rounded < 0, 2.0, 3.0))).astype(BF16)
    places = lax.broadcasted_iota(jnp.int32, (pool, ids.shape[1]), 0)
    chosen = jnp.where(places == ids, 1.0, 0.0).astype(BF16)
    picked = lax.dot_general(value, chosen, TN, preferred_element_type=F32)
    codes = lax.dot_general(code, chosen, TN, preferred_element_type=F32)
    special = jnp.where(codes == 1.0, jnp.inf, jnp.where(codes == 2.0, -jnp.inf, jnp.nan))
    return jnp.where(codes == 0.0, picked, special).astype(BF16)


def kernel(
    train_hbm, pool_hbm, kinv_hbm, ids_hbm, out_ref,
    kinv, train, turned, ids, pool, part1, got1, part2, got2, mine, precond, part3, got3, part4, got4,
    load_sem, pool_send, pool_recv, send1, recv1, send2, recv2, send3, recv3, send4, recv4, send5, recv5,
):
    g, d, f = lax.axis_index("groups"), lax.axis_index("dp"), lax.axis_index("feat")
    x, c = f // 2, f % 2
    depth, width = kinv.shape[1], kinv.shape[2]
    pool_rows = pool.shape[0] * pool.shape[1]
    sibling = (g, d, 2 * x + 1 - c)
    around = [(1 - g, 1 - x), (1 - g, x), (g, 1 - x), (g, x)]
    held = train.shape[2]

    def remote(src, dst, send, recv, device):
        return pltpu.make_async_remote_copy(
            src_ref=src, dst_ref=dst, send_sem=send, recv_sem=recv, device_id=device, device_id_type=MESH
        )

    loads = []

    def load(src, dst):
        copy = pltpu.make_async_copy(src, dst, load_sem.at[len(loads)])
        copy.start()
        loads.append(copy)
        return copy

    depth_from = pl.multiple_of(g * depth, depth)
    pool_half = pool_hbm.at[:, pl.ds(depth_from, depth)]
    own_pool = load(pool_half, pool.at[d])
    barrier = pltpu.get_barrier_semaphore()
    for r in range(1, 4):
        pl.semaphore_signal(barrier, inc=1, device_id=(g, (d + r) % 4, f), device_id_type=MESH)
    for r in range(4):
        for gg in (g, 1 - g) if r else (1 - g,):
            pl.semaphore_signal(barrier, inc=1, device_id=(gg, d, (f + r) % 4), device_id_type=MESH)

    train_loads = [
        load(
            train_hbm.at[pl.ds(i * train.shape[1], train.shape[1]), pl.ds(pl.multiple_of(g * held, held), held)],
            train.at[i],
        )
        for i in range(4)
    ]
    kinv_loads = []
    for i in range(8):
        core = 1 - c if i < 4 else c
        gg, xx = around[i % 4]
        col = pl.multiple_of((gg * 4 + 2 * xx + core) * width, width)
        kinv_loads.append(load(kinv_hbm.at[pl.ds(depth_from, depth), pl.ds(col, width)], kinv.at[i]))
    ids_load = load(ids_hbm, ids)

    pl.semaphore_wait(barrier, 10)

    own_pool.wait()
    outward = 1 - 2 * (d // 2)
    pool_copies = []
    for r in (3, 2, 1):
        target = (g, (d + 4 + outward * r) % 4, f)
        copy = remote(pool.at[d], pool.at[d], pool_send.at[r], pool_recv.at[d], target)
        copy.start()
        pool_copies.append(copy)
    for i in range(4):
        train_loads[i].wait()
        turned[i] = train[i].T
    for r in (1, 2, 3):
        source = (d + r) % 4
        remote(pool.at[source], pool.at[source], pool_send.at[r], pool_recv.at[source], sibling).wait_recv()
    rows = pool[...].reshape(pool_rows, depth)

    copies1 = []
    for i in range(4):
        kinv_loads[i].wait()
        part1[i] = jnp.dot(rows, kinv[i], preferred_element_type=F32)
        copy = remote(part1.at[i], got1.at[i], send1.at[i], recv1.at[i], sibling)
        copy.start()
        copies1.append(copy)
    copies2 = []
    for i in range(4):
        kinv_loads[4 + i].wait()
        term = jnp.dot(rows, kinv[4 + i], preferred_element_type=F32)
        copies1[i].wait_recv()
        both = term + got1[i]
        if i == 3:
            total = both
        else:
            part2[i] = both.astype(BF16)
        if i < 3:
            gg, xx = around[i]
            copy = remote(part2.at[i], got2.at[i], send2.at[i], recv2.at[i], (gg, d, 2 * xx + c))
            copy.start()
            copies2.append(copy)
    for i in (2, 1, 0):
        copies2[i].wait_recv()
        total = total + got2[i].astype(F32)
    mine[...] = total.astype(BF16)

    here = pl.multiple_of(f * width, width)
    copies3 = []
    for r in range(4):
        target = (g, (d + 4 + outward * r) % 4, d)
        copies3.append(remote(mine, precond.at[:, pl.ds(here, width)], send3.at[r], recv3.at[f], target))
    for r in (3, 2, 1):
        copies3[r].start()

    @pl.when(f != d)
    def _():
        copies3[0].start()

    @pl.when(f == d)
    def _():
        precond[:, pl.ds(here, width)] = mine[...]

    ids_load.wait()

    chunks = [2 * xx + cc for cc in (1 - c, c) for xx in (1 - x, x)]
    copies4 = []
    for r, source in enumerate((f, 2 * x + 1 - c, 2 * (1 - x) + c, 2 * (1 - x) + 1 - c)):
        columns = pl.ds(pl.multiple_of(source * width, width), width)
        arrival = remote(mine, precond.at[:, columns], send3.at[0], recv3.at[source], sibling)
        if r:
            arrival.wait_recv()
        else:
            pl.when(f != d)(arrival.wait_recv)
        left = precond[:, columns]
        for i, chunk in enumerate(chunks):
            more = jnp.dot(left, turned[chunk, columns, :], preferred_element_type=F32)
            if r == 0:
                part3[i] = more
            else:
                part3[i] = part3[i] + more
            if r == 3 and i < 2:
                copies4.append(remote(part3.at[i], got3.at[i], send4.at[i], recv4.at[i], sibling))
                copies4[i].start()
    copies5 = []
    for i in range(2):
        copies4[i].wait_recv()
        both = part3[2 + i] + got3[i]
        part4[i] = both.astype(BF16)
        for gg, xx in around[:1] + around[2:3] if i == 0 else around[1:2]:
            n = len(copies5)
            copy = remote(part4.at[i], got4.at[n], send5.at[n], recv5.at[n], (gg, d, 2 * xx + c))
            copy.start()
            copies5.append(copy)
    total = both
    for n in (2, 1, 0):
        copies5[n].wait_recv()
        total = total + got4[n].astype(F32)
    out_ref[...] = pick_columns(total, ids[...], pool_rows)

    for copy in pool_copies + copies1 + copies2 + copies3[1:] + copies4 + copies5:
        copy.wait_send()
    pl.when(f != d)(copies3[0].wait_send)


def fused(train_feats, pool_feats, kernel_inv, test_ids):
    rows, feats = train_feats.shape
    pool_block = pool_feats.shape[0]
    pool_rows = 4 * pool_block
    depth, width = feats // 2, kernel_inv.shape[1] // 8
    out_rows = rows // 4
    queries = test_ids.shape[0]
    dma = pltpu.SemaphoreType.DMA
    held_in_hbm = (train_feats, pool_feats, kernel_inv, test_ids.reshape(1, queries))
    return pl.pallas_call(
        kernel,
        out_shape=jax.ShapeDtypeStruct((out_rows, queries), BF16),
        in_specs=[pl.BlockSpec(memory_space=pl.ANY)] * 4,
        out_specs=pl.BlockSpec(memory_space=pltpu.VMEM),
        scratch_shapes=[
            pltpu.VMEM((8, depth, width), BF16),
            pltpu.VMEM((4, out_rows, depth), BF16),
            pltpu.VMEM((4, depth, out_rows), BF16),
            pltpu.VMEM((1, queries), jnp.int32),
            pltpu.VMEM((4, pool_block, depth), BF16),
            pltpu.VMEM((4, pool_rows, width), F32),
            pltpu.VMEM((4, pool_rows, width), F32),
            pltpu.VMEM((4, pool_rows, width), BF16),
            pltpu.VMEM((3, pool_rows, width), BF16),
            pltpu.VMEM((pool_rows, width), BF16),
            pltpu.VMEM((pool_rows, 4 * width), BF16),
            pltpu.VMEM((4, pool_rows, out_rows), F32),
            pltpu.VMEM((4, pool_rows, out_rows), F32),
            pltpu.VMEM((2, pool_rows, out_rows), BF16),
            pltpu.VMEM((3, pool_rows, out_rows), BF16),
            dma((14,)), dma((4,)), dma((4,)), dma((4,)), dma((4,)), dma((3,)), dma((3,)),
            dma((4,)), dma((4,)), dma((2,)), dma((2,)), dma((3,)), dma((3,)),
        ],
        compiler_params=pltpu.CompilerParams(
            collective_id=0, has_side_effects=True, vmem_limit_bytes=48 * 1024 * 1024
        ),
        cost_estimate=pl.CostEstimate(
            flops=2 * pool_rows * feats * (kernel_inv.shape[1] + rows) // 2,
            bytes_accessed=train_feats.size + kernel_inv.size + 2 * out_rows * queries,
            transcendentals=0,
        ),
    )(*[pltpu.with_memory_space_constraint(held, pltpu.HBM) for held in held_in_hbm])


def solution(mesh):
    sizes = tuple(mesh.shape[name] for name in ("groups", "dp", "feat"))

    def body(train_feats, pool_feats, kernel_inv, test_ids):
        pool_rows = sizes[1] * pool_feats.shape[0]
        square = train_feats.shape[1] == kernel_inv.shape[1]
        if sizes == (2, 4, 4) and square and pool_rows <= test_ids.shape[0]:
            return fused(train_feats, pool_feats, kernel_inv, test_ids)
        return per_device(train_feats, pool_feats, kernel_inv, test_ids)

    placed = (P("dp", "feat"), P("dp", "feat"), P("feat", "dp"), P("groups"))
    return jax.shard_map(
        body,
        mesh=mesh,
        in_specs=placed,
        out_specs=P(("dp", "feat"), "groups"),
        check_vma=False,
    )
```
